32 devices in a mesh: blk: 8 (over z, x), head: 4 (over y, core).
Axes of the slice: x: 2, y: 2, z: 4, core: 2. Of those that a mesh axis runs over, the one named last changes fastest.
Arguments:
- hidden: bfloat16 [1024, 2048], P('blk', 'head'), may hold values from -6 to 6
- key_cache: bfloat16 [1024, 1024], P('blk', 'head'), may hold values from -6 to 6
- value_cache: bfloat16 [1024, 1024], P('blk', 'head'), may hold values from -6 to 6
- block_spans: int32 [3], replicated, may hold values from 1 to 4, 8 in all
- cached_counts: int32 [8], replicated, may hold values from 0 to 128, as said below
- expert_ids: int32 [1024, 4], P('blk'), may hold values from 0 to 63, all different within a row; in each aligned block of 128 rows (0 to 127, 128 to 255, ...) at most 10 rows name the same one
- gate_weights: float32 [1024, 4], P('blk'), may hold values from 0.06 to 0.6
- attention_gain: float32 [2048], replicated, may hold values from 0.1 to 1.9
- mixture_gain: float32 [2048], replicated, may hold values from 0.1 to 1.9
- query_gain: float32 [128], replicated, may hold values from 0.1 to 1.9
- key_gain: float32 [128], replicated, may hold values from 0.1 to 1.9
- query_weight: bfloat16 [2048, 1024], P(None, 'head'), may hold values from -0.125 to 0.125
- key_weight: bfloat16 [2048, 1024], P(None, 'head'), may hold values from -0.125 to 0.125
- value_weight: bfloat16 [2048, 1024], P(None, 'head'), may hold values from -0.125 to 0.125
- output_weight: bfloat16 [1024, 2048], P('head', 'blk'), may hold values from -0.5 to 0.5
- expert_gate: bfloat16 [128, 2048, 512], P('blk', None, 'head'), may hold values from -0.125 to 0.125
- expert_up: bfloat16 [128, 2048, 512], P('blk', None, 'head'), may hold values from -0.125 to 0.125
- expert_down: bfloat16 [128, 512, 2048], P('blk', 'head'), may hold values from -0.1875 to 0.1875
Outputs:
- attention_out: bfloat16 [1024, 2048], P('blk', 'head')
- layer_out: bfloat16 [1024, 2048], P('blk', 'head')
The draws below stay inside these ranges and needn't reach their ends.
Inputs may be any that keep to these rules, and one draw needn't show every extreme that they name: `block_spans`: the requests occupy all 8 blocks together; some request occupies 4 blocks. `cached_counts`: live cache slots come first in a block; some block has all 128 live. `expert_ids`: A token's experts differ. In the rows of one block (128 tokens) no expert is named by more than 10 rows.
All inputs are finite; a program needn't handle non-finite values.
Results may differ from the reference program's by a relative error of at most 0.012.
Values may be sent and summed in bfloat16 or wider, within the bound.
A program may use at most 128 MiB of HBM per device.

```python
import math
import jax
import jax.numpy as jnp
import numpy as np
from jax import lax

D = 2048
HEADS = 8
HD = 128
EXPERTS = 64
FF = 1024
TOPK = 4
HP = 2
SPAN = 4
Q_DEV = 128
C_DEV = 128
TOKENS = 1024
CACHE = 1024
REQS = 3
CAP = 10
N_BLK = 8
N_HEAD = 4


def draw_cached_counts(key, part):
    first_key, second_key, third_key, fourth_key = jax.random.split(jax.random.fold_in(key, 11), 4)
    heavy_pick = jax.random.randint(first_key, (N_BLK,), 0, 3) == 0
    high_count = jax.random.randint(second_key, (N_BLK,), C_DEV * 3 // 4, C_DEV + 1)
    low_count = jax.random.randint(third_key, (N_BLK,), 0, C_DEV // 8 + 1)
    counts = jnp.where(heavy_pick, high_count, low_count)
    full_spot = jax.random.randint(fourth_key, (), 0, N_BLK)
    return jnp.where(jnp.arange(N_BLK) == full_spot, C_DEV, counts).astype(jnp.int32)


def level_of(rng, dims, cuts, least, largest):
    def one(dim, shards_of):
        draws = jax.random.uniform(jax.random.fold_in(jax.random.fold_in(rng, 6), dim), (shards_of,), jnp.float32, least / len(cuts), largest / len(cuts))
        return jnp.repeat(jnp.exp(draws), dims[dim] // shards_of).reshape((-1,) + (1,) * (len(dims) - dim - 1))

    factor_of = one(*cuts[0])
    for cut in cuts[1:]:
        factor_of = factor_of * one(*cut)
    return factor_of


def profile(amount, total, most, slope):
    portions = [(1 << 20) // math.isqrt(rank ** slope) + 1 for rank in range(2, amount + 1)]
    rest, holding = total - most - (amount - 1), [1] * (amount - 1)
    while rest > 0:
        candidates = [i for i in range(amount - 1) if holding[i] < most]
        mass, left = sum([portions[i] for i in candidates]), rest
        for i in candidates:
            addition = min(most - holding[i], max(1, left * portions[i] // mass), rest)
            holding[i] = holding[i] + addition
            rest = rest - addition
    return np.array([most] + holding)


def ragged_sizes(own_key, number_of, total, reach, skew):
    if number_of == 2:
        one = jax.random.randint(own_key, (), max(1, total - reach), min(reach, total - 1) + 1)
        return jnp.stack([one, total - one])
    lengths = jnp.asarray(profile(number_of, total, reach, skew), jnp.int32)
    pairs = (number_of - 1) // 2
    donor, receiver = lengths[1:1 + 2 * pairs:2], lengths[2:2 + 2 * pairs:2]
    slack = jnp.minimum(donor - 1, reach - receiver)
    passed = jax.random.randint(jax.random.fold_in(own_key, 1), (pairs,), 0, 1 << 20) % (slack + 1)
    lengths = lengths.at[1:1 + 2 * pairs:2].set(donor - passed).at[2:2 + 2 * pairs:2].set(receiver + passed)
    return lengths[jax.random.permutation(jax.random.fold_in(own_key, 2), number_of)]


def assign_block(rng, own, number, rows, number_of, top, bound, lean):
    ranking = jax.random.permutation(rng, number_of)
    heavy_load, usual = shares(number_of, rows * top, bound, lean, True), shares(number_of, rows * top, bound, lean, False)
    places = jnp.arange(number_of)

    def named(lengths, turn):
        used = int((lengths > 0).sum())
        fixed = max(1, used // 4)
        passed = fixed + (places - fixed + turn * (used - fixed)) % max(1, number_of - fixed)
        return jnp.zeros((number_of,), jnp.int32).at[ranking[jnp.where(places < fixed, places, passed)]].set(jnp.asarray(lengths, jnp.int32))

    lengths = jnp.where(number % 4 == 0, named(heavy_load, number // 4), named(usual, number - number // 4 - 1))
    mixed = jax.random.permutation(jax.random.fold_in(own, 3), number_of)
    source_of, receiver = mixed[0:number_of // 2 * 2:2], mixed[1:number_of // 2 * 2:2]
    slack = jnp.minimum(lengths[source_of] - 1, bound - lengths[receiver]) // 2
    slack = jnp.where((source_of == ranking[0]) | (receiver == ranking[0]) | (lengths[receiver] == 0), 0, jnp.maximum(slack, 0))
    passed = jax.random.randint(jax.random.fold_in(own, 4), (number_of // 2,), 0, 1 << 20) % (slack + 1)
    lengths = lengths.at[source_of].add(-passed).at[receiver].add(passed)
    items = jnp.searchsorted(jnp.cumsum(lengths), jnp.arange(rows * top), side="right").astype(jnp.int32)
    listing = items.reshape(top, rows).T
    listing = listing[jax.random.permutation(jax.random.fold_in(own, 1), rows)]
    turn = jax.random.randint(jax.random.fold_in(own, 2), (rows, 1), 0, top)
    return jnp.take_along_axis(listing, (jnp.arange(top)[None, :] + turn) % top, axis=1)


def shares(amount, total, most, slope, full):
    portions = [(1 << 20) // math.isqrt(standing ** slope) + 1 for standing in range(1, amount + 1)]
    largest = most if full else min(most, max(-(-total // amount), total * portions[0] // sum(portions)))
    least = 1 if total - largest >= amount - 1 else 0
    given, spare = [largest] + [least] * (amount - 1), total - largest - least * (amount - 1)
    while spare > 0:
        free = [i for i in range(1, amount) if given[i] < largest] or [i for i in range(1, amount) if given[i] < most]
        mass, remaining = sum([portions[i] for i in free]), spare
        for i in free:
            addition = min(most - given[i], max(1, remaining * portions[i] // mass), spare)
            given[i] = given[i] + addition
            spare = spare - addition
    return np.array(given)


def bell_draw(key, dims, scale, most, cuts=(), held_as=jnp.bfloat16):
    array = jax.random.normal(key, dims, jnp.float32) * scale
    if len(cuts) > 0:
        array = level_of(key, dims, cuts, -0.22, 0.18) * array
    return jnp.clip(array, min=-most, max=most).astype(held_as)


def setup_inputs(seed: int = 0) -> dict:
    keys = jax.random.split(jax.random.key(seed), 19)
    hidden = bell_draw(keys[0], (TOKENS, D), 1.0, 6.0, ((0, 8), (1, 4)))
    key_cache = bell_draw(keys[1], (CACHE, HEADS * HD), 1.0, 6.0, ((0, 8), (1, 4)))
    value_cache = bell_draw(keys[2], (CACHE, HEADS * HD), 1.0, 6.0, ((0, 8), (1, 4)))
    block_spans = ragged_sizes(keys[3], REQS, N_BLK, SPAN, 1).astype(jnp.int32)
    cached_counts = draw_cached_counts(jax.random.fold_in(keys[18], 71), 0)
    expert_ids_keys = jax.random.split(jax.random.fold_in(keys[5], 1), TOKENS // Q_DEV)
    expert_ids_turns = jax.random.permutation(jax.random.fold_in(keys[5], 3), TOKENS // Q_DEV)
    expert_ids = jax.vmap(lambda own, number: assign_block(jax.random.fold_in(keys[5], 2), own, number, Q_DEV, EXPERTS, TOPK, CAP, 1))(expert_ids_keys, expert_ids_turns).reshape((TOKENS, TOPK))
    gate_weights = jnp.clip(jnp.exp(math.log(0.6) - 2.3025852 * jax.random.uniform(keys[6], (TOKENS, TOPK), jnp.float32) ** level_of(keys[6], (TOKENS, TOPK), ((0, 8),), -0.2, 0.2)), 0.06, 0.6)
    attention_gain = jnp.clip(1.0 + 0.18 * jax.random.normal(keys[7], (D,), jnp.float32), 0.1, 1.9)
    mixture_gain = jnp.clip(1.0 + 0.18 * jax.random.normal(keys[8], (D,), jnp.float32), 0.1, 1.9)
    query_gain = jnp.clip(1.0 + 0.18 * jax.random.normal(keys[9], (HD,), jnp.float32), 0.1, 1.9)
    key_gain = jnp.clip(1.0 + 0.18 * jax.random.normal(keys[10], (HD,), jnp.float32), 0.1, 1.9)
    query_weight = bell_draw(keys[11], (D, HEADS * HD), D ** -0.5, 0.125, ((1, 4),))
    key_weight = bell_draw(keys[12], (D, HEADS * HD), D ** -0.5, 0.125, ((1, 4),))
    value_weight = bell_draw(keys[13], (D, HEADS * HD), D ** -0.5, 0.125, ((1, 4),))
    output_weight = bell_draw(keys[14], (HEADS * HD, D), HD ** -0.5, 0.5, ((0, 4), (1, 8)))
    expert_gate = bell_draw(keys[15], (EXPERTS * HP, D, FF // HP), D ** -0.5, 0.125, ((0, 8), (2, 4)))
    expert_up = bell_draw(keys[16], (EXPERTS * HP, D, FF // HP), D ** -0.5, 0.125, ((0, 8), (2, 4)))
    expert_down = bell_draw(keys[17], (EXPERTS * HP, FF // HP, D), FF ** -0.5, 0.1875, ((0, 8), (1, 4)))
    return {"hidden": hidden, "key_cache": key_cache, "value_cache": value_cache, "block_spans": block_spans, "cached_counts": cached_counts, "expert_ids": expert_ids, "gate_weights": gate_weights, "attention_gain": attention_gain, "mixture_gain": mixture_gain, "query_gain": query_gain, "key_gain": key_gain, "query_weight": query_weight, "key_weight": key_weight, "value_weight": value_weight, "output_weight": output_weight, "expert_gate": expert_gate, "expert_up": expert_up, "expert_down": expert_down}


def row_norm(values, gain_vector):
    return values * lax.rsqrt(lax.optimization_barrier(jnp.mean(values * values, axis=-1, keepdims=True)) + 1e-05) * gain_vector

def head_norm(projected, gain_vector):
    shaped = projected.reshape(projected.shape[0], -1, HD)
    normed = row_norm(shaped, gain_vector)
    return normed.reshape(projected.shape).astype(jnp.bfloat16)

def block_requests(block_spans):
    boundary = jnp.cumsum(block_spans)
    blocks = jnp.arange(N_BLK, dtype=jnp.int32)
    return lax.optimization_barrier(jnp.sum((blocks[:, None] >= boundary[None, :]).astype(jnp.int32), axis=1))

def attend(queries, key_rows, value_rows, allowed):
    head_count = queries.shape[1] // HD
    query_heads = queries.astype(jnp.float32).reshape(queries.shape[0], head_count, HD)
    key_heads = key_rows.astype(jnp.float32).reshape(key_rows.shape[0], head_count, HD)
    value_heads = value_rows.astype(jnp.float32).reshape(value_rows.shape[0], head_count, HD)
    scores = jnp.einsum('qhd,khd->hqk', query_heads, key_heads, precision=lax.Precision.HIGHEST) * HD ** (-0.5)
    weights = jnp.where(allowed[None, None, :], jnp.exp(scores), 0.0)
    denominator = lax.optimization_barrier(jnp.sum(weights, axis=2))
    rounded = lax.optimization_barrier(weights.astype(jnp.bfloat16))
    numerator = jnp.einsum('hqk,khd->hqd', rounded.astype(jnp.float32), value_heads, precision=lax.Precision.HIGHEST)
    context = numerator / denominator[:, :, None]
    return jnp.transpose(context, (1, 0, 2)).reshape(queries.shape[0], -1).astype(jnp.bfloat16)

def reference(hidden, key_cache, value_cache, block_spans, cached_counts, expert_ids, gate_weights, attention_gain, mixture_gain, query_gain, key_gain, query_weight, key_weight, value_weight, output_weight, expert_gate, expert_up, expert_down):
    hidden_wide = hidden.astype(jnp.float32)
    normed = row_norm(hidden_wide, attention_gain).astype(jnp.bfloat16)
    queries = head_norm(jnp.dot(normed, query_weight, preferred_element_type=jnp.float32), query_gain)
    new_keys = head_norm(jnp.dot(normed, key_weight, preferred_element_type=jnp.float32), key_gain)
    new_values = jnp.dot(normed, value_weight, preferred_element_type=jnp.float32).astype(jnp.bfloat16)
    old_keys = head_norm(key_cache.astype(jnp.float32), key_gain)
    feature_width = HEADS * HD
    block_keys = jnp.concatenate([old_keys.reshape(N_BLK, C_DEV, feature_width), new_keys.reshape(N_BLK, Q_DEV, feature_width)], axis=1)
    block_values = jnp.concatenate([value_cache.reshape(N_BLK, C_DEV, feature_width), new_values.reshape(N_BLK, Q_DEV, feature_width)], axis=1)
    live_slots = jnp.concatenate([jnp.arange(C_DEV, dtype=jnp.int32)[None, :] < cached_counts[:, None], jnp.ones((N_BLK, Q_DEV), jnp.bool_)], axis=1)
    requests = block_requests(block_spans)
    margin = SPAN - 1
    padded_keys = jnp.pad(block_keys, ((margin, margin), (0, 0), (0, 0)))
    padded_values = jnp.pad(block_values, ((margin, margin), (0, 0), (0, 0)))
    padded_live = jnp.pad(live_slots, ((margin, margin), (0, 0)))
    padded_requests = jnp.pad(requests, (margin, margin), constant_values=-1)

    def one_block(block_index):
        near_keys = lax.dynamic_slice_in_dim(padded_keys, block_index, 2 * SPAN - 1, 0).reshape(-1, feature_width)
        near_values = lax.dynamic_slice_in_dim(padded_values, block_index, 2 * SPAN - 1, 0).reshape(-1, feature_width)
        near_live = lax.dynamic_slice_in_dim(padded_live, block_index, 2 * SPAN - 1, 0)
        near_requests = lax.dynamic_slice_in_dim(padded_requests, block_index, 2 * SPAN - 1, 0)
        allowed = ((near_requests == requests[block_index])[:, None] & near_live).reshape(-1)
        own_queries = lax.dynamic_slice_in_dim(queries, block_index * Q_DEV, Q_DEV, 0)
        return attend(own_queries, near_keys, near_values, allowed)
    context = lax.map(one_block, jnp.arange(N_BLK, dtype=jnp.int32)).reshape(TOKENS, feature_width)
    attention = jnp.dot(context, output_weight, preferred_element_type=jnp.float32)
    attention_out = attention.astype(jnp.bfloat16)
    after_attention = hidden_wide + attention
    mixed_in = row_norm(after_attention, mixture_gain).astype(jnp.bfloat16)
    tokens_padded = jnp.concatenate([mixed_in, jnp.zeros((1, D), jnp.bfloat16)], axis=0)
    ids_padded = jnp.concatenate([expert_ids, jnp.full((1, TOPK), -1, jnp.int32)], axis=0)
    gates_padded = jnp.concatenate([gate_weights, jnp.zeros((1, TOPK), jnp.float32)], axis=0)
    quarter_width = FF // HP // N_HEAD

    def expert_step(running_sum, expert):
        chosen = jnp.any(expert_ids == expert, axis=1)
        picked = jnp.nonzero(chosen, size=N_BLK * CAP, fill_value=TOKENS)[0].astype(jnp.int32)
        token_rows = tokens_padded[picked]
        row_weight = lax.optimization_barrier(jnp.sum(jnp.where(ids_padded[picked] == expert, gates_padded[picked], 0.0), axis=1))
        summed = jnp.zeros((N_BLK * CAP, D), jnp.float32)
        for half_index in range(HP):
            slot_index = expert * HP + half_index
            gate_matrix = lax.dynamic_index_in_dim(expert_gate, slot_index, 0, keepdims=False)
            up_matrix = lax.dynamic_index_in_dim(expert_up, slot_index, 0, keepdims=False)
            down_matrix = lax.dynamic_index_in_dim(expert_down, slot_index, 0, keepdims=False)
            gate_part = jnp.dot(token_rows, gate_matrix, preferred_element_type=jnp.float32)
            up_part = jnp.dot(token_rows, up_matrix, preferred_element_type=jnp.float32)
            activation = (jax.nn.silu(gate_part) * up_part).astype(jnp.bfloat16)
            for quarter in range(N_HEAD):
                first_unit = quarter * quarter_width
                quarter_part = jnp.dot(activation[:, first_unit:first_unit + quarter_width], down_matrix[first_unit:first_unit + quarter_width], preferred_element_type=jnp.float32).astype(jnp.bfloat16)
                summed = summed + quarter_part.astype(jnp.float32)
        return (running_sum.at[picked].add(row_weight[:, None] * summed), None)
    mixture, _ = lax.scan(expert_step, jnp.zeros((TOKENS + 1, D), jnp.float32), jnp.arange(EXPERTS, dtype=jnp.int32))
    layer_out = (after_attention + mixture[:TOKENS]).astype(jnp.bfloat16)
    return (attention_out, layer_out)
```

```python
import functools

import jax
import jax.numpy as jnp
from jax import lax
from jax.experimental import pallas as pl
from jax.experimental.pallas import tpu as pltpu
from jax.sharding import PartitionSpec as P

HD = 128
EXPERTS = 64
TOPK = 4
HP = 2
SPAN = 4
CAP = 10
REACH = SPAN - 1
LANES = 128
F32 = jnp.float32
BF16 = jnp.bfloat16
MESH = pl.DeviceIdType.MESH
DISTANCES = (1, -1, 2, -2, 3, -3)


def dot(left, right):
    return jnp.dot(left, right, preferred_element_type=F32)


def head_norm(projected, gain):
    parts = []
    for first in range(0, projected.shape[1], HD):
        head = projected[:, first : first + HD]
        scale = lax.rsqrt(jnp.mean(head * head, axis=-1, keepdims=True) + 1e-05)
        parts.append((head * scale * gain).astype(BF16))
    return jnp.concatenate(parts, axis=1)


def attention_kernel(
    blocks, heads,
    hidden, key_cache, value_cache, attention_gain, query_gain, key_gain, mask,
    query_weight, key_weight, value_weight,
    context,
    rows, pairs, numerator, denominator,
    row_send, row_recv, pair_send, pair_recv,
):
    blk, head = lax.axis_index("blk"), lax.axis_index("head")
    inside = lambda block: (block >= 0) & (block < blocks)

    barrier = pltpu.get_barrier_semaphore()
    for step in range(1, heads):
        pl.semaphore_signal(
            barrier, inc=1, device_id=(blk, lax.rem(head + step, heads)), device_id_type=MESH
        )
    for distance in DISTANCES:
        @pl.when(inside(blk + distance))
        def _():
            pl.semaphore_signal(
                barrier, inc=1, device_id=(blk + distance, head), device_id_type=MESH
            )
    near = sum(jnp.where(inside(blk + distance), 1, 0) for distance in DISTANCES)
    pl.semaphore_wait(barrier, heads - 1 + near)

    def row_copy(step):
        return pltpu.make_async_remote_copy(
            src_ref=hidden, dst_ref=rows.at[head],
            send_sem=row_send.at[step], recv_sem=row_recv.at[head],
            device_id=(blk, lax.rem(head + step, heads)), device_id_type=MESH,
        )

    def row_arrival(source):
        return pltpu.make_async_remote_copy(
            src_ref=hidden, dst_ref=rows.at[source],
            send_sem=row_send.at[0], recv_sem=row_recv.at[source],
            device_id=(blk, source), device_id_type=MESH,
        )

    def pair_copy(distance, part):
        slot = distance + REACH
        return pltpu.make_async_remote_copy(
            src_ref=pairs.at[REACH, pl.ds(2 * part, 2)],
            dst_ref=pairs.at[slot, pl.ds(2 * part, 2)],
            send_sem=pair_send.at[slot, part], recv_sem=pair_recv.at[slot, part],
            device_id=(blk + distance, head), device_id_type=MESH,
        )

    for step in range(1, heads):
        row_copy(step).start()
    rows[head] = hidden[...]

    def send_pairs(part):
        for distance in DISTANCES:
            @pl.when(inside(blk + distance))
            def _():
                pair_copy(distance, part).start()

    pairs[REACH, 0] = head_norm(key_cache[...].astype(F32), key_gain[...])
    pairs[REACH, 1] = value_cache[...]
    send_pairs(0)

    for step in range(1, heads):
        row_arrival(lax.rem(head + step, heads)).wait_recv()
    width = hidden.shape[1]
    square = jnp.zeros((hidden.shape[0], 1), F32)
    for source in range(heads):
        piece = rows[source].astype(F32)
        square += jnp.sum(piece * piece, axis=-1, keepdims=True)
    scale = lax.rsqrt(square / (heads * width) + 1e-05)
    normed = jnp.concatenate(
        [
            (rows[source].astype(F32) * scale * attention_gain[:, source * width : (source + 1) * width]).astype(BF16)
            for source in range(heads)
        ],
        axis=1,
    )
    pairs[REACH, 2] = head_norm(dot(normed, key_weight[...]), key_gain[...])
    pairs[REACH, 3] = dot(normed, value_weight[...]).astype(BF16)
    send_pairs(1)
    queries = head_norm(dot(normed, query_weight[...]), query_gain[...])

    numerator[...] = jnp.zeros_like(numerator)
    denominator[...] = jnp.zeros_like(denominator)
    head_count = queries.shape[1] // HD

    def attend(slot, part):
        allowed = mask[slot, part] > 0.0
        for index in range(head_count):
            lanes = slice(index * HD, (index + 1) * HD)
            keys = pairs[slot, 2 * part][:, lanes]
            values = pairs[slot, 2 * part + 1][:, lanes]
            scores = lax.dot_general(
                queries[:, lanes], keys, (((1,), (1,)), ((), ())), preferred_element_type=F32
            ) * HD ** (-0.5)
            weights = jnp.where(allowed, jnp.exp(scores), 0.0)
            denominator[index] += jnp.sum(weights, axis=1, keepdims=True)
            numerator[index] += dot(weights.astype(BF16), values)

    attend(REACH, 0)
    attend(REACH, 1)
    for part in range(2):
        for distance in DISTANCES:
            @pl.when(inside(blk - distance))
            def _():
                pair_copy(distance, part).wait_recv()
                attend(distance + REACH, part)
    context[...] = jnp.concatenate(
        [numerator[index] / denominator[index] for index in range(head_count)], axis=1
    ).astype(BF16)
    for step in range(1, heads):
        row_copy(step).wait_send()
    for part in range(2):
        for distance in DISTANCES:
            @pl.when(inside(blk + distance))
            def _():
                pair_copy(distance, part).wait_send()


def mixture_kernel(
    blocks, heads, stride, merged,
    context, output_weight, hidden, dispatch, combine, mixture_gain,
    expert_gate, expert_up, expert_down,
    attention_out, layer_out,
    partial, arrived, after,
    outgoing, gathered, slabs, gates, ups, downs,
    pair_out, pair_in, cross_out, cross_in, back_out, back_in,
    share_send, share_recv, weight_sem,
    all_send, all_recv, core_send, core_recv, side_send, side_recv, relay_send, relay_recv,
    pair_send, pair_recv, cross_send, cross_recv, back_send, back_recv,
):
    blk, head = lax.axis_index("blk"), lax.axis_index("head")
    core_peer = head + 1 - 2 * lax.rem(head, 2)
    side_peer = lax.rem(head + 2, 4)
    far_peer = lax.rem(core_peer + 2, 4)
    room = outgoing.shape[1]
    width = hidden.shape[1]
    share = width // LANES
    groups = expert_gate.shape[0] // merged

    def remote(source, target, send, recv, where):
        return pltpu.make_async_remote_copy(
            src_ref=source, dst_ref=target, send_sem=send, recv_sem=recv,
            device_id=where, device_id_type=MESH,
        )

    def weight_copies(index):
        units = pl.ds(index * merged, merged)
        return [
            pltpu.make_async_copy(source.at[units], target.at[units], weight_sem.at[kind, index])
            for kind, (source, target) in enumerate(
                ((expert_gate, gates), (expert_up, ups), (expert_down, downs))
            )
        ]

    @pl.loop(0, groups)
    def _(index):
        for copy in weight_copies(index):
            copy.start()

    barrier = pltpu.get_barrier_semaphore()
    for step in range(1, heads):
        pl.semaphore_signal(
            barrier, inc=1, device_id=(blk, lax.rem(head + step, heads)), device_id_type=MESH
        )

    @pl.loop(1, blocks)
    def _(step):
        pl.semaphore_signal(
            barrier, inc=1, device_id=(lax.rem(blk + step, blocks), head), device_id_type=MESH
        )

    def share_copy(step):
        target = lax.rem(head + step, heads)
        return remote(
            partial.at[target], arrived.at[step], share_send.at[step], share_recv.at[step],
            (blk, target),
        )

    ctx = context[...]
    for index in range(heads):
        partial[index] = dot(ctx, output_weight[:, index * width : (index + 1) * width]).astype(BF16)
    pl.semaphore_wait(barrier, heads - 1 + blocks - 1)
    for step in range(1, heads):
        share_copy(step).start()
    total = partial[head].astype(F32)
    for step in range(1, heads):
        share_copy(step).wait_recv()
        total = total + arrived[step].astype(F32)
    attention_out[...] = total.astype(BF16)
    total = total + hidden[...].astype(F32)
    after[...] = total
    rounded = total.astype(BF16)

    def all_copy(step):
        target = lax.rem(blk + step, blocks)
        return remote(
            outgoing.at[target], gathered.at[head, blk], all_send.at[step], all_recv.at[step],
            (target, head),
        )

    def all_arrival(step):
        source = lax.rem(blk - step + blocks, blocks)
        return remote(
            outgoing.at[source], gathered.at[head, source], all_send.at[step], all_recv.at[step],
            (source, head),
        )

    def core_copy(source, step):
        return remote(
            gathered.at[head, source], gathered.at[head, source],
            core_send.at[step], core_recv.at[step], (blk, core_peer),
        )

    def side_copy(source, step):
        return remote(
            gathered.at[head, source], gathered.at[head, source],
            side_send.at[step], side_recv.at[step], (blk, side_peer),
        )

    def relay_copy(source, step):
        return remote(
            gathered.at[side_peer, source], gathered.at[side_peer, source],
            relay_send.at[step], relay_recv.at[step], (blk, core_peer),
        )

    def arrival(owner, source, send, recv):
        return remote(
            gathered.at[owner, source], gathered.at[owner, source], send, recv, (blk, core_peer)
        )

    @pl.loop(1, blocks)
    def _(step):
        target = lax.rem(blk + step, blocks)
        outgoing[target] = dot(dispatch[target], rounded).astype(BF16)
        all_copy(step).start()

    gathered[head, blk] = dot(dispatch[blk], rounded).astype(BF16)
    core_copy(blk, 0).start()
    side_copy(blk, 0).start()

    @pl.loop(1, blocks)
    def _(step):
        source = lax.rem(blk - step + blocks, blocks)
        all_arrival(step).wait_recv()
        core_copy(source, step).start()
        side_copy(source, step).start()

    @pl.loop(0, blocks)
    def _(step):
        source = lax.rem(blk - step + blocks, blocks)
        arrival(side_peer, source, side_send.at[step], side_recv.at[step]).wait_recv()
        relay_copy(source, step).start()

    @pl.loop(0, blocks)
    def _(step):
        source = lax.rem(blk - step + blocks, blocks)
        arrival(core_peer, source, core_send.at[step], core_recv.at[step]).wait_recv()
        arrival(far_peer, source, relay_send.at[step], relay_recv.at[step]).wait_recv()
        square = jnp.zeros((room, 1), F32)
        for index in range(heads):
            piece = gathered[index, source].astype(F32)
            square += jnp.sum(piece * piece, axis=-1, keepdims=True)
        scale = lax.rsqrt(square / (heads * width) + 1e-05)
        place = pl.ds(pl.multiple_of(source * room, 16), room)
        for index in range(heads):
            normed = gathered[index, source].astype(F32) * scale
            for lane in range(share):
                slab = index * share + lane
                slabs[slab, place, :] = (
                    normed[:, lane * LANES : (lane + 1) * LANES]
                    * mixture_gain[:, slab * LANES : (slab + 1) * LANES]
                )

    depth = heads * share

    @pl.loop(0, groups)
    def _(index):
        for copy in weight_copies(index):
            copy.wait()
        mine = pl.ds(index, blocks * room // stride, stride) if stride > 1 else pl.ds(0, blocks * room)
        tokens = jnp.concatenate(
            [slabs[slab, mine, :].astype(BF16) for slab in range(depth)], axis=1
        )
        units = [index * merged + unit for unit in range(merged)]
        gate = dot(tokens, jnp.concatenate([gates[unit] for unit in units], axis=1))
        up = dot(tokens, jnp.concatenate([ups[unit] for unit in units], axis=1))
        activation = (gate / (1.0 + jnp.exp(-gate)) * up).astype(BF16)
        for first in range(0, depth, 4):
            lanes = slice(first * LANES, (first + 4) * LANES)
            made = dot(activation, jnp.concatenate([downs[unit, :, lanes] for unit in units], axis=0))
            for lane in range(4):
                slabs[first + lane, mine, :] = made[:, lane * LANES : (lane + 1) * LANES]

    core_far = lax.rem(core_peer, 2)
    row = head // 2

    def slab_rows(owner, place):
        return jnp.concatenate([slabs[owner * share + lane, place, :] for lane in range(share)], axis=1)

    def pair_copy(target, step):
        return remote(
            pair_out.at[target], pair_in.at[target], pair_send.at[step], pair_recv.at[step],
            (blk, core_peer),
        )

    def cross_copy(target, step):
        return remote(
            cross_out.at[target], cross_in.at[target], cross_send.at[step], cross_recv.at[step],
            (blk, side_peer),
        )

    def back_copy(step):
        target = lax.rem(blk + step, blocks)
        return remote(
            back_out.at[target], back_in.at[blk], back_send.at[step], back_recv.at[step],
            (target, head),
        )

    def back_arrival(step):
        source = lax.rem(blk - step + blocks, blocks)
        return remote(
            back_out.at[source], back_in.at[source], back_send.at[step], back_recv.at[step],
            (source, head),
        )

    def each(body):
        @pl.loop(1, blocks + 1)
        def _(count):
            step = lax.rem(count, blocks)
            target = lax.rem(blk + step, blocks)
            body(target, step, pl.ds(pl.multiple_of(target * room, 16), room))

    def to_core(target, step, place):
        for side in range(2):
            pair_out[target, side] = slab_rows(2 * side + core_far, place).astype(BF16)
        pair_copy(target, step).start()

    def to_side(target, step, place):
        pair_copy(target, step).wait_recv()
        other = slab_rows(side_peer, place) + pair_in[target, 1 - row].astype(F32)
        cross_out[target] = other.astype(BF16)
        cross_copy(target, step).start()

    def final(target, place):
        return (
            slab_rows(head, place) + pair_in[target, row].astype(F32) + cross_in[target].astype(F32)
        ).astype(BF16)

    each(to_core)
    each(to_side)

    @pl.loop(1, blocks)
    def _(step):
        target = lax.rem(blk + step, blocks)
        place = pl.ds(pl.multiple_of(target * room, 16), room)
        cross_copy(target, step).wait_recv()
        back_out[target] = final(target, place)
        back_copy(step).start()

    cross_copy(blk, 0).wait_recv()
    back_in[blk] = final(blk, pl.ds(pl.multiple_of(blk * room, 16), room))

    def weighted(source):
        return sum(
            lax.dot_general(
                combine[half, source], back_in[source], (((0,), (0,)), ((), ())),
                preferred_element_type=F32,
            )
            for half in range(2)
        )

    after[...] += weighted(blk)

    @pl.loop(1, blocks)
    def _(step):
        source = lax.rem(blk - step + blocks, blocks)
        back_arrival(step).wait_recv()
        after[...] += weighted(source)

    layer_out[...] = after[...].astype(BF16)

    for step in range(1, heads):
        share_copy(step).wait_send()

    @pl.loop(1, blocks)
    def _(step):
        all_copy(step).wait_send()
        back_copy(step).wait_send()

    @pl.loop(0, blocks)
    def _(step):
        source = lax.rem(blk - step + blocks, blocks)
        target = lax.rem(blk + step, blocks)
        core_copy(source, step).wait_send()
        side_copy(source, step).wait_send()
        relay_copy(source, step).wait_send()
        pair_copy(target, step).wait_send()
        cross_copy(target, step).wait_send()


def local(
    hidden, key_cache, value_cache, block_spans, cached_counts, expert_ids, gate_weights,
    attention_gain, mixture_gain, query_gain, key_gain,
    query_weight, key_weight, value_weight, output_weight,
    expert_gate, expert_up, expert_down,
):
    blocks, heads = lax.axis_size("blk"), lax.axis_size("head")
    block_index = lax.axis_index("blk")
    tokens, width = hidden.shape
    slots = key_cache.shape[0]
    local_width = key_cache.shape[1]

    whole_output = lax.all_gather(output_weight, "blk", axis=1, tiled=True)

    requests = jnp.arange(block_spans.shape[0])
    boundary = jnp.sum(
        jnp.where(requests[None, :] <= requests[:, None], block_spans[None, :], 0), axis=1
    )
    sources = block_index - jnp.arange(-REACH, REACH + 1, dtype=jnp.int32)
    request_of = lambda block: jnp.sum(
        (block[..., None] >= boundary).astype(jnp.int32), axis=-1
    )
    same = (
        (sources >= 0) & (sources < blocks) & (request_of(sources) == request_of(block_index))
    )
    live_count = jnp.sum(
        jnp.where(sources[:, None] == jnp.arange(blocks)[None, :], cached_counts[None, :], 0), axis=1
    )
    old_live = jnp.arange(slots, dtype=jnp.int32)[None, :] < live_count[:, None]
    mask = jnp.stack(
        [same[:, None] & old_live, jnp.broadcast_to(same[:, None], (same.shape[0], tokens))], axis=1
    ).astype(F32)[:, :, None, :]

    vmem = pl.BlockSpec(memory_space=pltpu.VMEM)
    hbm = pl.BlockSpec(memory_space=pl.ANY)
    dma = pltpu.SemaphoreType.DMA
    context = pl.pallas_call(
        functools.partial(attention_kernel, blocks, heads),
        out_shape=jax.ShapeDtypeStruct((tokens, local_width), BF16),
        in_specs=[vmem] * 10,
        out_specs=vmem,
        scratch_shapes=[
            pltpu.VMEM((heads, tokens, width), BF16),
            pltpu.VMEM((2 * REACH + 1, 4, slots, local_width), BF16),
            pltpu.VMEM((local_width // HD, tokens, HD), F32),
            pltpu.VMEM((local_width // HD, tokens, 1), F32),
            dma((heads,)), dma((heads,)),
            dma((2 * REACH + 1, 2)), dma((2 * REACH + 1, 2)),
        ],
        compiler_params=pltpu.CompilerParams(
            collective_id=0, has_side_effects=True, vmem_limit_bytes=24 << 20
        ),
        name="attention",
    )(
        hidden, key_cache, value_cache, attention_gain[None, :], query_gain[None, :],
        key_gain[None, :], mask, query_weight, key_weight, value_weight,
    )

    held = expert_gate.shape[0]
    merged = HP if held % HP == 0 else 1
    stride = held // merged
    room = -(-stride * CAP // 16) * 16
    named = jnp.sum(
        (expert_ids[:, :, None] == jnp.arange(EXPERTS, dtype=jnp.int32)).astype(F32), axis=1
    )
    earlier = jnp.arange(tokens)[:, None] > jnp.arange(tokens)[None, :]
    ranks = dot(earlier.astype(BF16), named.astype(BF16))
    rank = jnp.sum(
        jnp.where(expert_ids[:, :, None] == jnp.arange(EXPERTS, dtype=jnp.int32), ranks[:, None, :], 0.0),
        axis=2,
    ).astype(jnp.int32)
    matches = []
    scaled = []
    spots = jnp.arange(blocks * room, dtype=jnp.int32)
    for copy in range(HP // merged):
        if merged == HP:
            spot = expert_ids // stride * room + rank * stride + expert_ids % stride
        else:
            unit = expert_ids * HP + copy
            spot = unit // stride * room + rank * stride + unit % stride
        for choice in range(TOPK):
            matches.append(spots[:, None] == spot[:, choice][None, :])
            scaled.append(
                jnp.where(spots[:, None] == spot[:, choice][None, :], gate_weights[:, choice][None, :], 0.0)
            )
    dispatch = sum(match.astype(F32) for match in matches).astype(BF16)
    weights = sum(scaled)
    high = lax.reduce_precision(weights, 8, 7)
    combine = jnp.stack([high, weights - high]).astype(BF16)
    combine = combine.reshape(2, blocks, room, tokens)
    dispatch = dispatch.reshape(blocks, room, tokens)

    features = heads * width
    units = expert_gate.shape[2]
    row_block = (blocks, room, width)
    return pl.pallas_call(
        functools.partial(mixture_kernel, blocks, heads, stride, merged),
        out_shape=(
            jax.ShapeDtypeStruct((tokens, width), BF16),
            jax.ShapeDtypeStruct((tokens, width), BF16),
        ),
        in_specs=[vmem] * 6 + [hbm] * 3,
        out_specs=(vmem, vmem),
        scratch_shapes=[
            pltpu.VMEM((heads, tokens, width), BF16),
            pltpu.VMEM((heads, tokens, width), BF16),
            pltpu.VMEM((tokens, width), F32),
            pltpu.VMEM(row_block, BF16),
            pltpu.VMEM((heads,) + row_block, BF16),
            pltpu.VMEM((features // LANES, blocks * room, LANES), F32),
            pltpu.VMEM((held, features, units), BF16),
            pltpu.VMEM((held, features, units), BF16),
            pltpu.VMEM((held, units, features), BF16),
            pltpu.VMEM((blocks, 2, room, width), BF16),
            pltpu.VMEM((blocks, 2, room, width), BF16),
            pltpu.VMEM(row_block, BF16),
            pltpu.VMEM(row_block, BF16),
            pltpu.VMEM(row_block, BF16),
            pltpu.VMEM(row_block, BF16),
            dma((heads,)), dma((heads,)), dma((3, stride)),
        ]
        + [dma((blocks,))] * 14,
        compiler_params=pltpu.CompilerParams(
            collective_id=1, has_side_effects=True, vmem_limit_bytes=56 << 20
        ),
        name="mixture",
    )(
        context, whole_output, hidden, dispatch, combine, mixture_gain[None, :],
        expert_gate, expert_up, expert_down,
    )


def solution(mesh):
    placed = (
        P("blk", "head"),
        P("blk", "head"),
        P("blk", "head"),
        P(),
        P(),
        P("blk", None),
        P("blk", None),
        P(),
        P(),
        P(),
        P(),
        P(None, "head"),
        P(None, "head"),
        P(None, "head"),
        P("head", "blk"),
        P("blk", None, "head"),
        P("blk", None, "head"),
        P("blk", "head", None),
    )
    return jax.shard_map(
        local,
        mesh=mesh,
        in_specs=placed,
        out_specs=(P("blk", "head"), P("blk", "head")),
        check_vma=False,
    )
```

```python
import functools

import jax
import jax.numpy as jnp
from jax import lax
from jax.experimental import pallas as pl
from jax.experimental.pallas import tpu as pltpu
from jax.sharding import PartitionSpec as P

HD = 128
EXPERTS = 64
TOPK = 4
HP = 2
SPAN = 4
CAP = 10
REACH = SPAN - 1
LANES = 128
F32 = jnp.float32
BF16 = jnp.bfloat16
MESH = pl.DeviceIdType.MESH
DISTANCES = (1, -1, 2, -2, 3, -3)


def dot(left, right):
    return jnp.dot(left, right, preferred_element_type=F32)


def head_norm(projected, gain):
    parts = []
    for first in range(0, projected.shape[1], HD):
        head = projected[:, first : first + HD]
        scale = lax.rsqrt(jnp.mean(head * head, axis=-1, keepdims=True) + 1e-05)
        parts.append((head * scale * gain).astype(BF16))
    return jnp.concatenate(parts, axis=1)


def attention_kernel(
    blocks, heads,
    hidden, key_cache, value_cache, attention_gain, query_gain, key_gain, mask,
    query_source, key_source, value_source,
    context,
    query_weight, key_weight, value_weight, weight_sem,
    rows, pairs, numerator, denominator,
    row_send, row_recv, pair_send, pair_recv,
):
    loads = [
        pltpu.make_async_copy(source, target, weight_sem.at[kind])
        for kind, (source, target) in enumerate(
            ((key_source, key_weight), (value_source, value_weight), (query_source, query_weight))
        )
    ]
    for load in loads:
        load.start()
    blk, head = lax.axis_index("blk"), lax.axis_index("head")
    inside = lambda block: (block >= 0) & (block < blocks)

    barrier = pltpu.get_barrier_semaphore()
    for step in range(1, heads):
        pl.semaphore_signal(
            barrier, inc=1, device_id=(blk, lax.rem(head + step, heads)), device_id_type=MESH
        )
    for distance in DISTANCES:
        @pl.when(inside(blk + distance))
        def _():
            pl.semaphore_signal(
                barrier, inc=1, device_id=(blk + distance, head), device_id_type=MESH
            )
    near = sum(jnp.where(inside(blk + distance), 1, 0) for distance in DISTANCES)
    pl.semaphore_wait(barrier, heads - 1 + near)

    def row_copy(step):
        return pltpu.make_async_remote_copy(
            src_ref=hidden, dst_ref=rows.at[head],
            send_sem=row_send.at[step], recv_sem=row_recv.at[head],
            device_id=(blk, lax.rem(head + step, heads)), device_id_type=MESH,
        )

    def row_arrival(source):
        return pltpu.make_async_remote_copy(
            src_ref=hidden, dst_ref=rows.at[source],
            send_sem=row_send.at[0], recv_sem=row_recv.at[source],
            device_id=(blk, source), device_id_type=MESH,
        )

    def pair_copy(distance, part):
        slot = distance + REACH
        return pltpu.make_async_remote_copy(
            src_ref=pairs.at[REACH, pl.ds(2 * part, 2)],
            dst_ref=pairs.at[slot, pl.ds(2 * part, 2)],
            send_sem=pair_send.at[slot, part], recv_sem=pair_recv.at[slot, part],
            device_id=(blk + distance, head), device_id_type=MESH,
        )

    for step in range(1, heads):
        row_copy(step).start()
    rows[head] = hidden[...]

    def send_pairs(part):
        for distance in DISTANCES:
            @pl.when(inside(blk + distance))
            def _():
                pair_copy(distance, part).start()

    pairs[REACH, 0] = head_norm(key_cache[...].astype(F32), key_gain[...])
    pairs[REACH, 1] = value_cache[...]
    send_pairs(0)

    for step in range(1, heads):
        row_arrival(lax.rem(head + step, heads)).wait_recv()
    width = hidden.shape[1]
    square = jnp.zeros((hidden.shape[0], 1), F32)
    for source in range(heads):
        piece = rows[source].astype(F32)
        square += jnp.sum(piece * piece, axis=-1, keepdims=True)
    scale = lax.rsqrt(square / (heads * width) + 1e-05)
    normed = jnp.concatenate(
        [
            (rows[source].astype(F32) * scale * attention_gain[:, source * width : (source + 1) * width]).astype(BF16)
            for source in range(heads)
        ],
        axis=1,
    )
    for load in loads:
        load.wait()
    pairs[REACH, 2] = head_norm(dot(normed, key_weight[...]), key_gain[...])
    pairs[REACH, 3] = dot(normed, value_weight[...]).astype(BF16)
    send_pairs(1)
    queries = head_norm(dot(normed, query_weight[...]), query_gain[...])

    numerator[...] = jnp.zeros_like(numerator)
    denominator[...] = jnp.zeros_like(denominator)
    head_count = queries.shape[1] // HD

    def attend(slot, part):
        allowed = mask[slot, part] > 0.0
        for index in range(head_count):
            lanes = slice(index * HD, (index + 1) * HD)
            keys = pairs[slot, 2 * part][:, lanes]
            values = pairs[slot, 2 * part + 1][:, lanes]
            scores = lax.dot_general(
                queries[:, lanes], keys, (((1,), (1,)), ((), ())), preferred_element_type=F32
            ) * HD ** (-0.5)
            weights = jnp.where(allowed, jnp.exp(scores), 0.0)
            denominator[index] += jnp.sum(weights, axis=1, keepdims=True)
            numerator[index] += dot(weights.astype(BF16), values)

    attend(REACH, 0)
    attend(REACH, 1)
    for part in range(2):
        for distance in DISTANCES:
            @pl.when(inside(blk - distance))
            def _():
                pair_copy(distance, part).wait_recv()
                attend(distance + REACH, part)
    context[...] = jnp.concatenate(
        [numerator[index] / denominator[index] for index in range(head_count)], axis=1
    ).astype(BF16)
    for step in range(1, heads):
        row_copy(step).wait_send()
    for part in range(2):
        for distance in DISTANCES:
            @pl.when(inside(blk + distance))
            def _():
                pair_copy(distance, part).wait_send()


def mixture_kernel(
    blocks, heads, stride, merged,
    context, output_weight, hidden, expert_ids, gate_weights, bases, mixture_gain,
    expert_gate, expert_up, expert_down,
    attention_out, layer_out,
    partial, arrived, after,
    outgoing, gathered, slabs, gates, ups, downs,
    pair_out, pair_in, cross_out, cross_in, back_out, back_in,
    share_send, share_recv, weight_sem,
    all_send, all_recv, core_send, core_recv, side_send, side_recv, relay_send, relay_recv,
    pair_send, pair_recv, cross_send, cross_recv, back_send, back_recv,
):
    blk, head = lax.axis_index("blk"), lax.axis_index("head")
    core_peer = head + 1 - 2 * lax.rem(head, 2)
    side_peer = lax.rem(head + 2, 4)
    far_peer = lax.rem(core_peer + 2, 4)
    room = outgoing.shape[1]
    width = hidden.shape[1]
    share = width // LANES
    groups = expert_gate.shape[0] // merged

    def remote(source, target, send, recv, where):
        return pltpu.make_async_remote_copy(
            src_ref=source, dst_ref=target, send_sem=send, recv_sem=recv,
            device_id=where, device_id_type=MESH,
        )

    def weight_copies(index):
        units = pl.ds(index * merged, merged)
        return [
            pltpu.make_async_copy(source.at[units], target.at[units], weight_sem.at[kind, index])
            for kind, (source, target) in enumerate(
                ((expert_gate, gates), (expert_up, ups), (expert_down, downs))
            )
        ]

    @pl.loop(0, groups)
    def _(index):
        for copy in weight_copies(index):
            copy.start()

    barrier = pltpu.get_barrier_semaphore()
    for step in range(1, heads):
        pl.semaphore_signal(
            barrier, inc=1, device_id=(blk, lax.rem(head + step, heads)), device_id_type=MESH
        )

    @pl.loop(1, blocks)
    def _(step):
        pl.semaphore_signal(
            barrier, inc=1, device_id=(lax.rem(blk + step, blocks), head), device_id_type=MESH
        )

    def share_copy(step):
        target = lax.rem(head + step, heads)
        return remote(
            partial.at[target], arrived.at[step], share_send.at[step], share_recv.at[step],
            (blk, target),
        )

    tokens = hidden.shape[0]
    experts = lax.broadcasted_iota(jnp.int32, (tokens, EXPERTS), 1)
    chosen = [expert_ids[:, choice : choice + 1] == experts for choice in range(TOPK)]
    named = sum(jnp.where(match, 1.0, 0.0) for match in chosen)
    earlier = lax.broadcasted_iota(jnp.int32, (tokens, tokens), 0) > lax.broadcasted_iota(
        jnp.int32, (tokens, tokens), 1
    )
    ranks = dot(jnp.where(earlier, 1.0, 0.0).astype(BF16), named.astype(BF16)) * stride
    spots = [
        (
            jnp.sum(jnp.where(chosen[choice], ranks + bases[copy : copy + 1, :], 0.0), axis=1, keepdims=True),
            gate_weights[:, choice : choice + 1],
        )
        for copy in range(HP // merged)
        for choice in range(TOPK)
    ]

    def slot_row(block):
        return (lax.broadcasted_iota(jnp.int32, (tokens, room), 1) + block * room).astype(F32)

    def dispatched(block, values):
        row = slot_row(block)
        match = sum(jnp.where(spot == row, 1.0, 0.0) for spot, _ in spots).astype(BF16)
        return lax.dot_general(
            match, values, (((0,), (0,)), ((), ())), preferred_element_type=F32
        ).astype(BF16)

    ctx = context[...]
    for index in range(heads):
        partial[index] = dot(ctx, output_weight[:, index * width : (index + 1) * width]).astype(BF16)
    pl.semaphore_wait(barrier, heads - 1 + blocks - 1)
    for step in range(1, heads):
        share_copy(step).start()
    total = partial[head].astype(F32)
    for step in range(1, heads):
        share_copy(step).wait_recv()
        total = total + arrived[step].astype(F32)
    attention_out[...] = total.astype(BF16)
    total = total + hidden[...].astype(F32)
    after[...] = total
    rounded = total.astype(BF16)

    def all_copy(step):
        target = lax.rem(blk + step, blocks)
        return remote(
            outgoing.at[target], gathered.at[head, blk], all_send.at[step], all_recv.at[step],
            (target, head),
        )

    def all_arrival(step):
        source = lax.rem(blk - step + blocks, blocks)
        return remote(
            outgoing.at[source], gathered.at[head, source], all_send.at[step], all_recv.at[step],
            (source, head),
        )

    def core_copy(source, step):
        return remote(
            gathered.at[head, source], gathered.at[head, source],
            core_send.at[step], core_recv.at[step], (blk, core_peer),
        )

    def side_copy(source, step):
        return remote(
            gathered.at[head, source], gathered.at[head, source],
            side_send.at[step], side_recv.at[step], (blk, side_peer),
        )

    def relay_copy(source, step):
        return remote(
            gathered.at[side_peer, source], gathered.at[side_peer, source],
            relay_send.at[step], relay_recv.at[step], (blk, core_peer),
        )

    def arrival(owner, source, send, recv):
        return remote(
            gathered.at[owner, source], gathered.at[owner, source], send, recv, (blk, core_peer)
        )

    @pl.loop(1, blocks)
    def _(step):
        target = lax.rem(blk + step, blocks)
        outgoing[target] = dispatched(target, rounded)
        all_copy(step).start()

    gathered[head, blk] = dispatched(blk, rounded)
    core_copy(blk, 0).start()
    side_copy(blk, 0).start()

    @pl.loop(1, blocks)
    def _(step):
        source = lax.rem(blk - step + blocks, blocks)
        all_arrival(step).wait_recv()
        core_copy(source, step).start()
        side_copy(source, step).start()

    @pl.loop(0, blocks)
    def _(step):
        source = lax.rem(blk - step + blocks, blocks)
        arrival(side_peer, source, side_send.at[step], side_recv.at[step]).wait_recv()
        relay_copy(source, step).start()

    @pl.loop(0, blocks)
    def _(step):
        source = lax.rem(blk - step + blocks, blocks)
        arrival(core_peer, source, core_send.at[step], core_recv.at[step]).wait_recv()
        arrival(far_peer, source, relay_send.at[step], relay_recv.at[step]).wait_recv()
        square = jnp.zeros((room, 1), F32)
        for index in range(heads):
            piece = gathered[index, source].astype(F32)
            square += jnp.sum(piece * piece, axis=-1, keepdims=True)
        scale = lax.rsqrt(square / (heads * width) + 1e-05)
        place = pl.ds(pl.multiple_of(source * room, 16), room)
        for index in range(heads):
            normed = gathered[index, source].astype(F32) * scale
            for lane in range(share):
                slab = index * share + lane
                slabs[slab, place, :] = (
                    normed[:, lane * LANES : (lane + 1) * LANES]
                    * mixture_gain[:, slab * LANES : (slab + 1) * LANES]
                )

    depth = heads * share

    @pl.loop(0, groups)
    def _(index):
        for copy in weight_copies(index):
            copy.wait()
        mine = pl.ds(index, blocks * room // stride, stride) if stride > 1 else pl.ds(0, blocks * room)
        tokens = jnp.concatenate(
            [slabs[slab, mine, :].astype(BF16) for slab in range(depth)], axis=1
        )
        units = [index * merged + unit for unit in range(merged)]
        gate = dot(tokens, jnp.concatenate([gates[unit] for unit in units], axis=1))
        up = dot(tokens, jnp.concatenate([ups[unit] for unit in units], axis=1))
        activation = (gate / (1.0 + jnp.exp(-gate)) * up).astype(BF16)
        for first in range(0, depth, 4):
            lanes = slice(first * LANES, (first + 4) * LANES)
            made = dot(activation, jnp.concatenate([downs[unit, :, lanes] for unit in units], axis=0))
            for lane in range(4):
                slabs[first + lane, mine, :] = made[:, lane * LANES : (lane + 1) * LANES]

    core_far = lax.rem(core_peer, 2)
    row = head // 2

    def slab_rows(owner, place):
        return jnp.concatenate([slabs[owner * share + lane, place, :] for lane in range(share)], axis=1)

    def pair_copy(target, step):
        return remote(
            pair_out.at[target], pair_in.at[target], pair_send.at[step], pair_recv.at[step],
            (blk, core_peer),
        )

    def cross_copy(target, step):
        return remote(
            cross_out.at[target], cross_in.at[target], cross_send.at[step], cross_recv.at[step],
            (blk, side_peer),
        )

    def back_copy(step):
        target = lax.rem(blk + step, blocks)
        return remote(
            back_out.at[target], back_in.at[blk], back_send.at[step], back_recv.at[step],
            (target, head),
        )

    def back_arrival(step):
        source = lax.rem(blk - step + blocks, blocks)
        return remote(
            back_out.at[source], back_in.at[source], back_send.at[step], back_recv.at[step],
            (source, head),
        )

    def each(body):
        @pl.loop(1, blocks + 1)
        def _(count):
            step = lax.rem(count, blocks)
            target = lax.rem(blk + step, blocks)
            body(target, step, pl.ds(pl.multiple_of(target * room, 16), room))

    def to_core(target, step, place):
        for side in range(2):
            pair_out[target, side] = slab_rows(2 * side + core_far, place).astype(BF16)
        pair_copy(target, step).start()

    def to_side(target, step, place):
        pair_copy(target, step).wait_recv()
        other = slab_rows(side_peer, place) + pair_in[target, 1 - row].astype(F32)
        cross_out[target] = other.astype(BF16)
        cross_copy(target, step).start()

    def final(target, place):
        return (
            slab_rows(head, place) + pair_in[target, row].astype(F32) + cross_in[target].astype(F32)
        ).astype(BF16)

    each(to_core)
    each(to_side)

    @pl.loop(1, blocks)
    def _(step):
        target = lax.rem(blk + step, blocks)
        place = pl.ds(pl.multiple_of(target * room, 16), room)
        cross_copy(target, step).wait_recv()
        back_out[target] = final(target, place)
        back_copy(step).start()

    cross_copy(blk, 0).wait_recv()
    back_in[blk] = final(blk, pl.ds(pl.multiple_of(blk * room, 16), room))

    def weighted(source):
        row = slot_row(source)
        weights = sum(jnp.where(spot == row, weight, 0.0) for spot, weight in spots)
        high = weights.astype(BF16)
        low = (weights - high.astype(F32)).astype(BF16)
        return dot(high, back_in[source]) + dot(low, back_in[source])

    after[...] += weighted(blk)

    @pl.loop(1, blocks)
    def _(step):
        source = lax.rem(blk - step + blocks, blocks)
        back_arrival(step).wait_recv()
        after[...] += weighted(source)

    layer_out[...] = after[...].astype(BF16)

    for step in range(1, heads):
        share_copy(step).wait_send()

    @pl.loop(1, blocks)
    def _(step):
        all_copy(step).wait_send()
        back_copy(step).wait_send()

    @pl.loop(0, blocks)
    def _(step):
        source = lax.rem(blk - step + blocks, blocks)
        target = lax.rem(blk + step, blocks)
        core_copy(source, step).wait_send()
        side_copy(source, step).wait_send()
        relay_copy(source, step).wait_send()
        pair_copy(target, step).wait_send()
        cross_copy(target, step).wait_send()


def local(
    hidden, key_cache, value_cache, block_spans, cached_counts, expert_ids, gate_weights,
    attention_gain, mixture_gain, query_gain, key_gain,
    query_weight, key_weight, value_weight, output_weight,
    expert_gate, expert_up, expert_down,
):
    blocks, heads = lax.axis_size("blk"), lax.axis_size("head")
    block_index = lax.axis_index("blk")
    tokens, width = hidden.shape
    slots = key_cache.shape[0]
    local_width = key_cache.shape[1]

    whole_output = lax.all_gather(output_weight, "blk", axis=1, tiled=True)

    requests = jnp.arange(block_spans.shape[0])
    boundary = jnp.sum(
        jnp.where(requests[None, :] <= requests[:, None], block_spans[None, :], 0), axis=1
    )
    sources = block_index - jnp.arange(-REACH, REACH + 1, dtype=jnp.int32)
    request_of = lambda block: jnp.sum(
        (block[..., None] >= boundary).astype(jnp.int32), axis=-1
    )
    same = (
        (sources >= 0) & (sources < blocks) & (request_of(sources) == request_of(block_index))
    )
    live_count = jnp.sum(
        jnp.where(sources[:, None] == jnp.arange(blocks)[None, :], cached_counts[None, :], 0), axis=1
    )
    old_live = jnp.arange(slots, dtype=jnp.int32)[None, :] < live_count[:, None]
    mask = jnp.stack(
        [same[:, None] & old_live, jnp.broadcast_to(same[:, None], (same.shape[0], tokens))], axis=1
    ).astype(F32)[:, :, None, :]

    vmem = pl.BlockSpec(memory_space=pltpu.VMEM)
    hbm = pl.BlockSpec(memory_space=pl.ANY)
    dma = pltpu.SemaphoreType.DMA
    context = pl.pallas_call(
        functools.partial(attention_kernel, blocks, heads),
        out_shape=jax.ShapeDtypeStruct((tokens, local_width), BF16),
        in_specs=[vmem] * 7 + [hbm] * 3,
        out_specs=vmem,
        scratch_shapes=[
            pltpu.VMEM(query_weight.shape, BF16),
            pltpu.VMEM(key_weight.shape, BF16),
            pltpu.VMEM(value_weight.shape, BF16),
            dma((3,)),
            pltpu.VMEM((heads, tokens, width), BF16),
            pltpu.VMEM((2 * REACH + 1, 4, slots, local_width), BF16),
            pltpu.VMEM((local_width // HD, tokens, HD), F32),
            pltpu.VMEM((local_width // HD, tokens, 1), F32),
            dma((heads,)), dma((heads,)),
            dma((2 * REACH + 1, 2)), dma((2 * REACH + 1, 2)),
        ],
        compiler_params=pltpu.CompilerParams(
            collective_id=0, has_side_effects=True, vmem_limit_bytes=56 << 20
        ),
        name="attention",
    )(
        hidden, key_cache, value_cache, attention_gain[None, :], query_gain[None, :],
        key_gain[None, :], mask, query_weight, key_weight, value_weight,
    )

    held = expert_gate.shape[0]
    merged = HP if held % HP == 0 else 1
    stride = held // merged
    room = -(-stride * CAP // 16) * 16
    unit = jnp.arange(EXPERTS)[None, :] * (HP // merged) + jnp.arange(HP // merged)[:, None]
    bases = (unit // stride * room + unit % stride).astype(F32)

    features = heads * width
    units = expert_gate.shape[2]
    row_block = (blocks, room, width)
    return pl.pallas_call(
        functools.partial(mixture_kernel, blocks, heads, stride, merged),
        out_shape=(
            jax.ShapeDtypeStruct((tokens, width), BF16),
            jax.ShapeDtypeStruct((tokens, width), BF16),
        ),
        in_specs=[vmem] * 7 + [hbm] * 3,
        out_specs=(vmem, vmem),
        scratch_shapes=[
            pltpu.VMEM((heads, tokens, width), BF16),
            pltpu.VMEM((heads, tokens, width), BF16),
            pltpu.VMEM((tokens, width), F32),
            pltpu.VMEM(row_block, BF16),
            pltpu.VMEM((heads,) + row_block, BF16),
            pltpu.VMEM((features // LANES, blocks * room, LANES), F32),
            pltpu.VMEM((held, features, units), BF16),
            pltpu.VMEM((held, features, units), BF16),
            pltpu.VMEM((held, units, features), BF16),
            pltpu.VMEM((blocks, 2, room, width), BF16),
            pltpu.VMEM((blocks, 2, room, width), BF16),
            pltpu.VMEM(row_block, BF16),
            pltpu.VMEM(row_block, BF16),
            pltpu.VMEM(row_block, BF16),
            pltpu.VMEM(row_block, BF16),
            dma((heads,)), dma((heads,)), dma((3, stride)),
        ]
        + [dma((blocks,))] * 14,
        compiler_params=pltpu.CompilerParams(
            collective_id=1, has_side_effects=True, vmem_limit_bytes=56 << 20
        ),
        name="mixture",
    )(
        context, whole_output, hidden, expert_ids, gate_weights, bases, mixture_gain[None, :],
        expert_gate, expert_up, expert_down,
    )


def solution(mesh):
    placed = (
        P("blk", "head"),
        P("blk", "head"),
        P("blk", "head"),
        P(),
        P(),
        P("blk", None),
        P("blk", None),
        P(),
        P(),
        P(),
        P(),
        P(None, "head"),
        P(None, "head"),
        P(None, "head"),
        P("head", "blk"),
        P("blk", None, "head"),
        P("blk", None, "head"),
        P("blk", "head", None),
    )
    return jax.shard_map(
        local,
        mesh=mesh,
        in_specs=placed,
        out_specs=(P("blk", "head"), P("blk", "head")),
        check_vma=False,
    )
```
